32 devices in a mesh: groups: 2 (over y), ctx: 4 (over z), tp: 4 (over x, core).
Axes of the slice: x: 2, y: 2, z: 4, core: 2. Of those that a mesh axis runs over, the one named last changes fastest.
Arguments:
- query_rows: bfloat16 [1024, 4096], P(('groups', 'ctx'), 'tp'), parts along dimension 0, may hold values from -36 to 36
- key_rows: bfloat16 [1024, 1024], P(('groups', 'ctx'), 'tp'), parts along dimension 0, may hold values from -9 to 9
- value_rows: bfloat16 [1024, 1024], P(('groups', 'ctx'), 'tp'), parts along dimension 0, may hold values from -6 to 6
- residual: bfloat16 [1024, 4096], P(('groups', 'ctx'), 'tp'), parts along dimension 0, may hold values from -6 to 6
- out_weight: bfloat16 [4096, 4096], P('tp', 'ctx'), may hold values from -0.09375 to 0.09375
- norm_gain: bfloat16 [4096], P('tp'), may hold values from 0.099609375 to 1.8984375
- query_weight: bfloat16 [4096, 4096], P('tp', 'ctx'), may hold values from -0.09375 to 0.09375
- key_value_weight: bfloat16 [4096, 2048], P('tp', 'ctx'), may hold values from -0.09375 to 0.09375
- token_types: int32 [1024], P('groups'), parts along dimension 0, may hold values from 0 to 1
- keep_list: int32 [1024], P('groups'), parts along dimension 0, may hold values from 0 to 1, as said below
- position_ids: int32 [3, 1024], P(None, 'groups'), parts along dimension 1, may hold values from 0 to 511
Outputs:
- kept_resid: bfloat16 [256, 4096], P(('groups', 'ctx'), 'tp'), parts along dimension 0
- attended_three: bfloat16 [256, 4096], P(('groups', 'ctx'), 'tp'), parts along dimension 0
The draws below stay inside these ranges and needn't reach their ends.
There are 2 independent parts, one for each index of `groups`. The reference program is written for one: setup_inputs(seed, part) draws one part's arguments, and reference() takes and returns one part's arrays. A program takes and returns all parts, laid end to end along the dimension named above; an argument that names none is the same for every part. Nothing has to cross between parts.
Inputs may be any that keep to these rules, and one draw needn't show every extreme that they name: keep_list is 0 at text tokens; exactly 128 tokens are text or kept, and all text tokens fit among them.
All inputs are finite; a program needn't handle non-finite values.
Results may differ from the reference program's by a relative error of at most 0.01.
Values may be sent and summed in bfloat16 or wider, within the bound.
A program may use at most 64 MiB of HBM per device.

```python
import math
import jax
import jax.numpy as jnp
from jax import lax

D = 4096
HEADS = 32
KV_HEADS = 8
HD = 128
TOK_DEV = 128
TOKENS = 512
KEPT = 128


def layout(key):
    key_pre, key_post, key_perm, key_level, key_extra, key_spot = jax.random.split(key, 6)
    prefix = jax.random.randint(key_pre, (), 1, TOKENS // 16 + 1)
    suffix = jax.random.randint(key_post, (), 1, TOKENS // 16 + 1)
    extra_count = jax.random.randint(key_extra, (), 0, TOKENS // 16 + 1)
    spots = jax.random.permutation(key_spot, TOKENS).astype(jnp.int32)
    spot_rank = jnp.argsort(spots, stable=True).astype(jnp.int32)
    token_index = jnp.arange(TOKENS, dtype=jnp.int32)
    is_text = (token_index < prefix) | (token_index >= TOKENS - suffix) | (spot_rank < extra_count)
    type_values = jnp.where(is_text, 0, 1).astype(jnp.int32)
    shuffled = jax.random.permutation(key_perm, TOKENS).astype(jnp.int32)
    block_level = jnp.repeat(jax.random.randint(key_level, (TOKENS // TOK_DEV,), 0, 4), TOK_DEV)
    priority = jnp.where(is_text, -1, shuffled + TOKENS * block_level)
    ranking = jnp.argsort(jnp.argsort(-priority, stable=True), stable=True)
    wanted = KEPT - jnp.sum(is_text.astype(jnp.int32))
    kept_visual = (~is_text & (ranking < wanted)).astype(jnp.int32)
    offset = token_index - prefix
    time_pos = prefix + offset // 256
    height_pos = prefix + offset // 16 % 16
    width_pos = prefix + offset % 16
    text_pos = token_index
    positions = jnp.stack([jnp.where(is_text, text_pos, time_pos), jnp.where(is_text, text_pos, height_pos), jnp.where(is_text, text_pos, width_pos)]).astype(jnp.int32)
    return (type_values, kept_visual, positions)


def attention_inputs(key):
    key_query, key_key = jax.random.split(key)
    queries = jnp.clip(jax.random.normal(key_query, (TOKENS, HEADS, HD), jnp.float32), -4.0, 4.0)
    key_block = jnp.clip(jax.random.normal(key_key, (TOKENS, KV_HEADS, HD), jnp.float32), -4.0, 4.0)
    token_index = jnp.arange(TOKENS)
    aligned_rows = token_index % 61 == 7
    next_one = jnp.roll(aligned_rows, -1)[:, None, None]
    next_two = jnp.roll(aligned_rows, -2)[:, None, None]
    key_block = jnp.where(next_one, key_block, jnp.where(next_two, 0.985 * jnp.roll(key_block, -1, axis=0), key_block))
    queries = jnp.where(aligned_rows[:, None, None], queries, queries)
    return (queries.reshape(TOKENS, HEADS * HD), key_block.reshape(TOKENS, KV_HEADS * HD))


def draw_query_rows(key, part):
    queries, key_block = attention_inputs(key)
    return queries.astype(jnp.bfloat16)


def draw_key_rows(key, part):
    queries, key_block = attention_inputs(key)
    return key_block.astype(jnp.bfloat16)


def draw_token_types(key, part):
    return layout(key)[0]


def draw_keep_list(key, part):
    return layout(key)[1]


def draw_position_ids(key, part):
    return layout(key)[2]


def level_of(own_key, extent, pieces, least, top_value):
    level, own = 1.0, jax.random.fold_in(own_key, 6)
    for axis_at, shards_of in pieces:
        draws = jnp.exp(jax.random.uniform(jax.random.fold_in(own, axis_at), (shards_of,), jnp.float32, least / len(pieces), top_value / len(pieces)))
        level = level * jnp.repeat(draws, extent[axis_at] // shards_of).reshape([-1 if axis == axis_at else 1 for axis in range(len(extent))])
    return level


def normal_values(rng, dims, deviation, bound, cuts=(), kind=jnp.bfloat16):
    values = jax.random.normal(rng, dims, jnp.float32) * deviation
    if len(cuts) > 0:
        values = level_of(rng, dims, cuts, -0.22, 0.18) * values
    return jnp.clip(values, min=-bound, max=bound).astype(kind)


def setup_inputs(seed: int = 0, part: int = 0) -> dict:
    key_list = jax.random.split(jax.random.key(seed), 12)
    part_keys = jax.random.split(jax.random.fold_in(key_list[11], part), 12)
    return {
        "query_rows": draw_query_rows(jax.random.fold_in(jax.random.fold_in(key_list[11], part), 71), part),
        "key_rows": draw_key_rows(jax.random.fold_in(jax.random.fold_in(key_list[11], part), 71), part),
        "value_rows": normal_values(part_keys[2], (TOKENS, KV_HEADS * HD), 1.0, 6.0, ((0, 4), (1, 4))),
        "residual": normal_values(part_keys[3], (TOKENS, D), 1.0, 6.0, ((0, 4), (1, 4))),
        "out_weight": normal_values(key_list[4], (HEADS * HD, D), (HEADS * HD) ** -0.5, 0.09375, ((0, 4), (1, 4))),
        "norm_gain": jnp.clip(1.0 + 0.18 * jax.random.normal(key_list[5], (D,), jnp.float32), 0.099609375, 1.8984375).astype(jnp.bfloat16),
        "query_weight": normal_values(key_list[6], (D, HEADS * HD), D ** -0.5, 0.09375, ((0, 4), (1, 4))),
        "key_value_weight": normal_values(key_list[7], (D, 2 * KV_HEADS * HD), D ** -0.5, 0.09375, ((0, 4), (1, 4))),
        "token_types": draw_token_types(jax.random.fold_in(jax.random.fold_in(key_list[11], part), 71), part),
        "keep_list": draw_keep_list(jax.random.fold_in(jax.random.fold_in(key_list[11], part), 71), part),
        "position_ids": draw_position_ids(jax.random.fold_in(jax.random.fold_in(key_list[11], part), 71), part),
    }


def rope_angles(positions):
    half_dim = HD // 2
    frequency = jnp.arange(half_dim, dtype=jnp.float32)
    inverse = jnp.exp(frequency * (-2.0 * math.log(1000000.0) / HD))
    section = jnp.where(frequency < HD // 8, 0, jnp.where(frequency < HD // 8 + 3 * HD // 16, 1, 2)).astype(jnp.int32)
    chosen = jnp.take(positions, section, axis=0).astype(jnp.float32)
    return chosen.T * inverse[None, :]

def rotate(states, angles):
    half_dim = HD // 2
    cosine = jnp.cos(angles)[:, None, :]
    sine_part = jnp.sin(angles)[:, None, :]
    leading = states[..., :half_dim]
    trailing = states[..., half_dim:]
    return jnp.concatenate([leading * cosine - trailing * sine_part, trailing * cosine + leading * sine_part], axis=-1)

def causal_attention(queries, key_block, value_block):
    row_count = queries.shape[0]
    head_count = queries.shape[1] // HD
    pair_count = key_block.shape[1] // HD
    group_size = head_count // pair_count
    query_heads = queries.reshape(row_count, head_count, HD).transpose(1, 0, 2)
    key_heads = key_block.reshape(row_count, pair_count, HD).transpose(1, 0, 2)
    value_heads = value_block.reshape(row_count, pair_count, HD).transpose(1, 0, 2)
    allowed = jnp.arange(row_count)[:, None] >= jnp.arange(row_count)[None, :]

    def one_head(head):
        pair_index = head // group_size
        scores = jnp.dot(query_heads[head], key_heads[pair_index].T, preferred_element_type=jnp.float32) * HD ** (-0.5)
        scores = jnp.where(allowed, scores, -1e+30)
        row_max = lax.optimization_barrier(jnp.max(scores, axis=1, keepdims=True))
        probs = jnp.where(allowed, jnp.exp(scores - row_max), 0.0)
        denominator = lax.optimization_barrier(jnp.sum(probs, axis=1, keepdims=True))
        return jnp.dot(probs.astype(jnp.bfloat16), value_heads[pair_index], preferred_element_type=jnp.float32) / denominator
    result = lax.map(one_head, jnp.arange(head_count, dtype=jnp.int32))
    return result.transpose(1, 0, 2).reshape(row_count, head_count * HD).astype(jnp.bfloat16)

def reference(query_rows, key_rows, value_rows, residual, out_weight, norm_gain, query_weight, key_value_weight, token_types, keep_list, position_ids):
    kept_flags = (token_types == 0) | (keep_list == 1)
    source = jnp.nonzero(kept_flags, size=KEPT)[0].astype(jnp.int32)
    attended = causal_attention(query_rows, key_rows, value_rows)
    hidden = (residual.astype(jnp.float32) + jnp.dot(attended, out_weight, preferred_element_type=jnp.float32)).astype(jnp.bfloat16)
    kept_resid = jnp.take(hidden, source, axis=0)
    mean_square = lax.optimization_barrier(jnp.mean(jnp.square(kept_resid.astype(jnp.float32)), axis=1, keepdims=True))
    normed = (kept_resid.astype(jnp.float32) * lax.rsqrt(mean_square + 1e-06) * norm_gain.astype(jnp.float32)[None, :]).astype(jnp.bfloat16)
    query_proj = jnp.dot(normed, query_weight, preferred_element_type=jnp.float32)
    pair_proj = jnp.dot(normed, key_value_weight, preferred_element_type=jnp.float32).reshape(KEPT, KV_HEADS, 2, HD)
    angles = rope_angles(jnp.take(position_ids, source, axis=1))
    query_three = rotate(query_proj.reshape(KEPT, HEADS, HD), angles).reshape(KEPT, HEADS * HD).astype(jnp.bfloat16)
    key_three = rotate(pair_proj[:, :, 0], angles).reshape(KEPT, KV_HEADS * HD).astype(jnp.bfloat16)
    value_three = pair_proj[:, :, 1].reshape(KEPT, KV_HEADS * HD).astype(jnp.bfloat16)
    return (kept_resid, causal_attention(query_three, key_three, value_three))
```

```python
import math

import jax
import jax.numpy as jnp
from jax import lax
from jax.experimental import pallas as pl
from jax.experimental.pallas import tpu as pltpu
from jax.sharding import PartitionSpec as P

D = 4096
HD = 128
KEPT_DEV = 32


neg_large = -1e30


def rope_angles(positions):
    half_dim = HD // 2
    frequency = jnp.arange(half_dim, dtype=jnp.float32)
    inverse = jnp.exp(frequency * (-2.0 * math.log(1000000.0) / HD))
    section = jnp.where(
        frequency < HD // 8, 0, jnp.where(frequency < HD // 8 + 3 * HD // 16, 1, 2)
    ).astype(jnp.int32)
    chosen = jnp.take(positions, section, axis=0).astype(jnp.float32)
    return chosen.T * inverse[None, :]


def rotate(states, angles):
    half_dim = HD // 2
    cosine = jnp.cos(angles)[:, None, :]
    sine_part = jnp.sin(angles)[:, None, :]
    leading = states[..., :half_dim]
    trailing = states[..., half_dim:]
    return jnp.concatenate(
        [leading * cosine - trailing * sine_part, trailing * cosine + leading * sine_part], axis=-1
    )


def attend(queries, key_block, value_block):
    row_count = queries.shape[0]
    pair_local = key_block.shape[1] // HD
    group_size = queries.shape[1] // HD // pair_local
    grouped = queries.reshape(row_count, pair_local, group_size, HD)
    query_index = lax.axis_index("ctx") * row_count + jnp.arange(row_count, dtype=jnp.int32)
    score_scale = HD ** (-0.5)
    key_piece = lax.all_gather(key_block, "ctx", axis=0, tiled=True)
    value_piece = lax.all_gather(value_block, "ctx", axis=0, tiled=True)
    key_count = key_piece.shape[0]
    key_heads = key_piece.reshape(key_count, pair_local, HD)
    value_heads = value_piece.reshape(key_count, pair_local, HD)
    scores = (
        jnp.einsum("tkgd,nkd->kgtn", grouped, key_heads, preferred_element_type=jnp.float32)
        * score_scale
    )
    key_index = jnp.arange(key_count, dtype=jnp.int32)
    allowed = key_index[None, :] <= query_index[:, None]
    scores = jnp.where(allowed, scores, neg_large)
    running = jnp.full((pair_local, group_size, row_count), neg_large, jnp.float32)
    newest = jnp.maximum(running, jnp.max(scores, axis=-1))
    probs = jnp.where(allowed, jnp.exp(scores - newest[..., None]), 0.0)
    denominator = jnp.sum(probs, axis=-1)
    accum = jnp.einsum(
        "kgtn,nkd->kgtd",
        probs.astype(jnp.bfloat16),
        value_heads,
        preferred_element_type=jnp.float32,
    )
    running, denominator, accum = (newest, denominator, accum)
    result = accum / denominator[..., None]
    return result.transpose(2, 0, 1, 3).reshape(row_count, -1).astype(jnp.bfloat16)


def project(row_block, weights):
    row_total = row_block.shape[0]
    shard_count = lax.axis_size("ctx")
    tensor_count = lax.axis_size("tp")
    widths = [matrix.shape[1] for matrix in weights]
    width_sum = sum(widths)
    combined = weights[0] if len(weights) == 1 else jnp.concatenate(weights, axis=1)
    update = jnp.dot(
        row_block,
        lax.all_gather(combined, "ctx", axis=1, tiled=True),
        preferred_element_type=jnp.float32,
    )
    arranged = update.reshape(row_total, shard_count, width_sum)
    member_blocks = []
    offset = 0
    for width in widths:
        member = arranged[:, :, offset : offset + width].reshape(
            row_total, tensor_count, shard_count * width // tensor_count
        )
        member_blocks.append(member)
        offset += width
    stacked = jnp.concatenate(member_blocks, axis=2).reshape(row_total, -1)
    own_share = lax.psum_scatter(stacked, "tp", scatter_dimension=1, tiled=True)
    results = []
    offset = 0
    for width in widths:
        share_width = shard_count * width // tensor_count
        results.append(own_share[:, offset : offset + share_width])
        offset += share_width
    return results


def relocate(row_block, source, first_row):
    row_total = row_block.shape[0]
    shard_count = lax.axis_size("ctx")
    local_index = source - first_row
    present = (local_index >= 0) & (local_index < row_total)
    picked = jnp.take(row_block, jnp.clip(local_index, 0, row_total - 1), axis=0)
    outgoing = jnp.where(present[:, None], picked, jnp.zeros_like(picked))
    incoming = lax.all_to_all(outgoing, "ctx", split_axis=0, concat_axis=0, tiled=True)
    slot_count = incoming.shape[0] // shard_count
    return jnp.sum(
        incoming.reshape(shard_count, slot_count, -1).astype(jnp.float32), axis=0
    ).astype(jnp.bfloat16)


def on_device(
    query_rows,
    key_rows,
    value_rows,
    residual,
    out_weight,
    norm_gain,
    query_weight,
    key_value_weight,
    token_types,
    keep_list,
    position_ids,
):
    shard_count = lax.axis_size("ctx")
    shard_index = lax.axis_index("ctx")
    local_rows = query_rows.shape[0]
    kept_flags = ((token_types == 0) | (keep_list == 1)).astype(jnp.int32)
    running_count = jnp.cumsum(kept_flags)
    slot_numbers = jnp.arange(KEPT_DEV * shard_count, dtype=jnp.int32) + 1
    source = jnp.searchsorted(running_count, slot_numbers, side="left")
    attended = attend(query_rows, key_rows, value_rows)
    first_row = shard_index * local_rows
    summed = project(attended, [out_weight])[0]
    hidden = (residual.astype(jnp.float32) + summed).astype(jnp.bfloat16)
    kept_resid = relocate(hidden, source, first_row)
    squares = lax.psum(jnp.sum(jnp.square(kept_resid.astype(jnp.float32)), axis=1), "tp")
    normed = (
        kept_resid.astype(jnp.float32)
        * lax.rsqrt(squares[:, None] / D + 1e-06)
        * norm_gain.astype(jnp.float32)[None, :]
    ).astype(jnp.bfloat16)
    query_proj, pair_proj = project(normed, [query_weight, key_value_weight])
    kept_count = normed.shape[0]
    own_source = lax.dynamic_slice_in_dim(source, shard_index * kept_count, kept_count)
    angles = rope_angles(jnp.take(position_ids, own_source, axis=1))
    query_three = (
        rotate(query_proj.reshape(kept_count, -1, HD), angles)
        .reshape(kept_count, -1)
        .astype(jnp.bfloat16)
    )
    pair_heads = pair_proj.reshape(kept_count, -1, 2, HD)
    key_three = rotate(pair_heads[:, :, 0], angles).reshape(kept_count, -1).astype(jnp.bfloat16)
    value_three = pair_heads[:, :, 1].reshape(kept_count, -1).astype(jnp.bfloat16)
    return (kept_resid, attend(query_three, key_three, value_three))

MESH = pl.DeviceIdType.MESH
N = 4


def shifted(index, step):
    return lax.rem(index + step, N)


def block_of(index, size):
    return pl.ds(pl.multiple_of(index * size, size), size)


def softmax_pair(queries, keys, values, allowed):
    scores = lax.dot_general(
        queries, keys, (((1,), (1,)), ((), ())), preferred_element_type=jnp.float32
    ) * (HD ** (-0.5))
    scores = jnp.where(allowed, scores, neg_large)
    probs = jnp.exp(scores - jnp.max(scores, axis=1, keepdims=True))
    denominator = jnp.sum(probs, axis=1, keepdims=True)
    gained = jnp.dot(probs.astype(jnp.bfloat16), values, preferred_element_type=jnp.float32)
    return (gained / denominator).astype(jnp.bfloat16)


def fused_kernel(
    query_ref, key_ref, value_ref, resid_ref, out_w_ref, gain_ref, query_w_ref, pair_w_ref,
    types_ref, keep_ref, pos_ref,
    kept_out, att_out,
    q_all, k_all, v_all, r_in, out_w, query_w, pair_w, pick, cos_s, sin_s,
    att_all, part, part_b, part_in, hid_own, hid_all,
    q_part, pair_part, sq_part, q_in, pair_in, sq_in, o_own, o_in,
    w_sem, own_sem, s1, r1, s_res, r_res, s2, r2, s3, r3, s4, r4, s5, r5, s6, r6,
):
    g, c, t = lax.axis_index("groups"), lax.axis_index("ctx"), lax.axis_index("tp")
    rows = query_ref.shape[0]
    tokens = q_all.shape[0]
    kept = pick.shape[0]
    share = kept // N
    f32, bf16 = jnp.float32, jnp.bfloat16

    def send(source, target, s_sem, r_sem, cc, tt):
        return pltpu.make_async_remote_copy(
            src_ref=source, dst_ref=target, send_sem=s_sem, recv_sem=r_sem,
            device_id=(g, cc, tt), device_id_type=MESH,
        )

    barrier = pltpu.get_barrier_semaphore()
    for dc in range(N):
        for dt in range(N):
            if dc or dt:
                pl.semaphore_signal(
                    barrier, inc=1, device_id=(g, shifted(c, dc), shifted(t, dt)),
                    device_id_type=MESH,
                )
    weights = [
        pltpu.make_async_copy(a, b, w_sem.at[i])
        for i, (a, b) in enumerate([(out_w_ref, out_w), (query_w_ref, query_w), (pair_w_ref, pair_w)])
    ]
    here = block_of(c, rows)
    arrays = [(query_ref, q_all, 2 * HD, 1), (key_ref, k_all, HD, 2), (value_ref, v_all, HD, 2)]
    own = [
        pltpu.make_async_copy(a.at[:, block_of(c // div, width)], b.at[here], own_sem.at[i])
        for i, (a, b, width, div) in enumerate(arrays)
    ]
    for copy in own:
        copy.start()
    pl.semaphore_wait(barrier, N * N - 1)

    first = []
    for d in (2, 1, 3):
        to = shifted(c, d)
        for i, (a, b, width, div) in enumerate(arrays):
            first.append(send(
                a.at[:, block_of(to // div, width)], b.at[here],
                s1.at[3 * (d - 1) + i], r1.at[3 * (d - 1) + i], to, t,
            ))
            first[-1].start()
    resid_copy = send(resid_ref, r_in, s_res, r_res, t, c)

    @pl.when(t != c)
    def _():
        resid_copy.start()

    resid_own = pltpu.make_async_copy(resid_ref, r_in, own_sem.at[3])

    @pl.when(t == c)
    def _():
        resid_own.start()

    for copy in weights:
        copy.start()

    flags = jnp.where((types_ref[...] == 0) | (keep_ref[...] == 1), 1.0, 0.0)
    before = lax.broadcasted_iota(jnp.int32, (tokens, tokens), 0) <= lax.broadcasted_iota(
        jnp.int32, (tokens, tokens), 1
    )
    counts = jnp.dot(
        jnp.broadcast_to(flags, (16, tokens)).astype(bf16),
        jnp.where(before, 1.0, 0.0).astype(bf16),
        preferred_element_type=f32,
    )[0:1]
    place = lax.broadcasted_iota(jnp.int32, (kept, tokens), 0).astype(f32) + 1.0
    chosen = jnp.where((counts == place) & (flags > 0.5), 1.0, 0.0)
    pick[...] = chosen.astype(bf16)
    token = lax.broadcasted_iota(jnp.int32, (kept, tokens), 1)
    source = jnp.sum(chosen * token.astype(f32), axis=1, keepdims=True)
    lane = lax.broadcasted_iota(jnp.int32, (1, HD), 1)
    freq = lax.rem(lane, HD // 2).astype(f32)
    inverse = jnp.exp(freq * (-2.0 * math.log(1000000.0) / HD))
    at = [
        jnp.sum(chosen * pos_ref[i : i + 1, :].astype(f32), axis=1, keepdims=True) for i in range(3)
    ]
    angle = jnp.where(freq < HD // 8, at[0], jnp.where(freq < HD // 8 + 3 * HD // 16, at[1], at[2]))
    angle = angle * inverse
    cos_s[...] = jnp.cos(angle)
    sin_s[...] = jnp.where(lane < HD // 2, -1.0, 1.0) * jnp.sin(angle)
    allowed = token.astype(f32) <= source
    allowed = jnp.concatenate([allowed, allowed], axis=0)

    for copy in own:
        copy.wait()
    for copy in first:
        copy.wait_recv()
    queries = jnp.dot(pick[...], q_all[...], preferred_element_type=f32).astype(bf16)
    queries = jnp.concatenate([queries[:, :HD], queries[:, HD:]], axis=0)
    attended = softmax_pair(queries, k_all[...], v_all[...], allowed)
    att_all[c, :, :HD] = attended[:kept]
    att_all[c, :, HD:] = attended[kept:]

    second = []
    for d in (2, 1, 3):
        second.append(send(att_all.at[c], att_all.at[c], s2.at[d - 1], r2.at[d - 1], shifted(c, d), t))
        second[-1].start()

    @pl.when(t != c)
    def _():
        resid_copy.wait_recv()

    @pl.when(t == c)
    def _():
        resid_own.wait()

    weights[0].wait()
    part[...] = jnp.dot(pick[:, block_of(t, rows)], r_in[...], preferred_element_type=f32)
    part[...] += jnp.dot(att_all[c], out_w[block_of(c, 2 * HD), :], preferred_element_type=f32)
    for copy, d in zip(second, (2, 1, 3)):
        copy.wait_recv()
    for d in (1, 3, 2):
        other = shifted(c, N - d)
        part[...] += jnp.dot(att_all[other], out_w[block_of(other, 2 * HD), :], preferred_element_type=f32)
    part_b[...] = part[...].astype(bf16)

    third = []
    for d in (2, 3, 1):
        to = shifted(t, d)
        third.append(send(part_b.at[block_of(to, share)], part_in.at[d - 1], s3.at[d - 1], r3.at[d - 1], c, to))
        third[-1].start()
    hidden = part[block_of(t, share), :]
    for copy in third:
        copy.wait_recv()
    for d in range(N - 1):
        hidden = hidden + part_in[d].astype(f32)
    hid_own[...] = hidden.astype(bf16)

    fourth = []
    for d in range(N):
        to = shifted(c, d)
        fourth.append(send(hid_own, hid_all.at[t], s4.at[d], r4.at[t], to, c))
    for d in (2, 1, 3):
        fourth[d].start()

    @pl.when(t != c)
    def _():
        fourth[0].start()

    @pl.when(t == c)
    def _():
        hid_all[t] = hid_own[...]

    weights[1].wait()
    weights[2].wait()
    for k in range(N):
        @pl.when((t != c) | (t != k))
        def _(k=k):
            send(hid_own, hid_all.at[k], s4.at[k], r4.at[k], c, t).wait_recv()

    kept_out[...] = hid_all[c]
    resid = hid_all[...].reshape(kept, hid_all.shape[2]).astype(f32)
    scaled = (resid * gain_ref[...].astype(f32)).astype(bf16)
    squares = jnp.sum(jnp.square(resid), axis=1, keepdims=True)
    sq_part[...] = jnp.broadcast_to(squares, (kept, HD)).T[:8]
    projected = jnp.dot(scaled, query_w[...], preferred_element_type=f32).astype(bf16)
    for i in range(N):
        q_part[i] = projected[:, 2 * HD * i : 2 * HD * (i + 1)]
    projected = jnp.dot(scaled, pair_w[...], preferred_element_type=f32).astype(bf16)
    for i in range(2):
        pair_part[i] = projected[:, 2 * HD * i : 2 * HD * (i + 1)]

    fifth = []
    for d in (2, 3, 1):
        to = shifted(t, d)
        for i, (a, b) in enumerate([
            (q_part.at[to], q_in.at[d - 1]), (pair_part.at[to // 2], pair_in.at[d - 1]),
            (sq_part, sq_in.at[d - 1]),
        ]):
            fifth.append(send(a, b, s5.at[3 * (d - 1) + i], r5.at[3 * (d - 1) + i], c, to))
            fifth[-1].start()
    query = q_part[t].astype(f32)
    pair = pair_part[t // 2].astype(f32)
    squares = sq_part[...]
    for copy in fifth:
        copy.wait_recv()
    for d in range(N - 1):
        query = query + q_in[d].astype(f32)
        pair = pair + pair_in[d].astype(f32)
        squares = squares + sq_in[d]
    total = jnp.broadcast_to(squares[0:1], (kept, HD)).T
    scale = lax.rsqrt(total / D + 1e-06)
    cosine, sine = cos_s[...] * scale, sin_s[...] * scale

    def turned(head):
        return (head * cosine + pltpu.roll(head, HD // 2, 1) * sine).astype(bf16)

    queries = jnp.concatenate([turned(query[:, :HD]), turned(query[:, HD:])], axis=0)
    row = lax.broadcasted_iota(jnp.int32, (kept, kept), 0)
    column = lax.broadcasted_iota(jnp.int32, (kept, kept), 1)
    causal = column <= row
    causal = jnp.concatenate([causal, causal], axis=0)
    values = (pair[:, HD:] * scale).astype(bf16)
    attended = softmax_pair(queries, turned(pair[:, :HD]), values, causal)
    o_own[:, :HD] = attended[:kept]
    o_own[:, HD:] = attended[kept:]

    sixth = []
    for d in range(N):
        to = shifted(c, d)
        sixth.append(send(o_own.at[block_of(to, share)], o_in.at[t], s6.at[d], r6.at[t], to, c))
    for d in (2, 1, 3):
        sixth[d].start()

    @pl.when(t != c)
    def _():
        sixth[0].start()

    @pl.when(t == c)
    def _():
        o_in[t] = o_own[block_of(c, share), :]

    for copies in (first, second, third, fifth, fourth[1:], sixth[1:]):
        for copy in copies:
            copy.wait_send()

    @pl.when(t != c)
    def _():
        resid_copy.wait_send()
        fourth[0].wait_send()
        sixth[0].wait_send()

    for k in range(N):
        @pl.when((t != c) | (t != k))
        def _(k=k):
            send(o_own.at[block_of(c, share)], o_in.at[k], s6.at[k], r6.at[k], c, t).wait_recv()

        att_out[:, 2 * HD * k : 2 * HD * (k + 1)] = o_in[k]


def fused(
    query_rows, key_rows, value_rows, residual, out_weight, norm_gain, query_weight,
    key_value_weight, token_types, keep_list, position_ids,
):
    rows, width = query_rows.shape
    tokens = rows * N
    kept = KEPT_DEV * N
    bf16, f32 = jnp.bfloat16, jnp.float32
    dma = pltpu.SemaphoreType.DMA
    vmem, anywhere = pl.BlockSpec(memory_space=pltpu.VMEM), pl.BlockSpec(memory_space=pl.ANY)
    scratch = [
        ((tokens, 2 * HD), bf16), ((tokens, HD), bf16), ((tokens, HD), bf16), (residual.shape, bf16),
        (out_weight.shape, bf16), (query_weight.shape, bf16), (key_value_weight.shape, bf16),
        ((kept, tokens), bf16), ((kept, HD), f32), ((kept, HD), f32),
        ((N, kept, 2 * HD), bf16), ((kept, width), f32), ((kept, width), bf16),
        ((N - 1, KEPT_DEV, width), bf16), ((KEPT_DEV, width), bf16), ((N, KEPT_DEV, width), bf16),
        ((N, kept, 2 * HD), bf16), ((2, kept, 2 * HD), bf16), ((8, HD), f32),
        ((N - 1, kept, 2 * HD), bf16), ((N - 1, kept, 2 * HD), bf16), ((N - 1, 8, HD), f32),
        ((kept, 2 * HD), bf16), ((N, KEPT_DEV, 2 * HD), bf16),
    ]
    counts = [(3,), (4,), (9,), (9,), (), (), (3,), (3,), (3,), (3,), (4,), (4,), (9,), (9,), (4,), (4,)]
    return pl.pallas_call(
        fused_kernel,
        out_shape=[jax.ShapeDtypeStruct((KEPT_DEV, width), bf16)] * 2,
        in_specs=[anywhere] * 5 + [vmem] + [anywhere] * 2 + [vmem] * 3,
        out_specs=[vmem, vmem],
        scratch_shapes=[pltpu.VMEM(s, d) for s, d in scratch]
        + [dma(n) if n else dma for n in counts],
        compiler_params=pltpu.CompilerParams(
            collective_id=0, has_side_effects=True, vmem_limit_bytes=48 * 1024 * 1024
        ),
    )(
        query_rows, key_rows, value_rows, residual, out_weight, norm_gain.reshape(1, -1),
        query_weight, key_value_weight, token_types.reshape(1, -1), keep_list.reshape(1, -1),
        position_ids,
    )


def solution(mesh):
    in_specs = (
        P(("groups", "ctx"), "tp"),
        P(("groups", "ctx"), "tp"),
        P(("groups", "ctx"), "tp"),
        P(("groups", "ctx"), "tp"),
        P("tp", "ctx"),
        P("tp"),
        P("tp", "ctx"),
        P("tp", "ctx"),
        P("groups"),
        P("groups"),
        P(None, "groups"),
    )
    out_specs = (P(("groups", "ctx"), "tp"), P(("groups", "ctx"), "tp"))
    whole_heads = mesh.shape["ctx"] == N and mesh.shape["tp"] == N
    return jax.shard_map(
        fused if whole_heads else on_device, mesh=mesh, in_specs=in_specs, out_specs=out_specs, check_vma=False
    )
```

```python
import math

import jax
import jax.numpy as jnp
from jax import lax
from jax.experimental import pallas as pl
from jax.experimental.pallas import tpu as pltpu
from jax.sharding import PartitionSpec as P

D = 4096
HD = 128
KEPT_DEV = 32


neg_large = -1e30


def rope_angles(positions):
    half_dim = HD // 2
    frequency = jnp.arange(half_dim, dtype=jnp.float32)
    inverse = jnp.exp(frequency * (-2.0 * math.log(1000000.0) / HD))
    section = jnp.where(
        frequency < HD // 8, 0, jnp.where(frequency < HD // 8 + 3 * HD // 16, 1, 2)
    ).astype(jnp.int32)
    chosen = jnp.take(positions, section, axis=0).astype(jnp.float32)
    return chosen.T * inverse[None, :]


def rotate(states, angles):
    half_dim = HD // 2
    cosine = jnp.cos(angles)[:, None, :]
    sine_part = jnp.sin(angles)[:, None, :]
    leading = states[..., :half_dim]
    trailing = states[..., half_dim:]
    return jnp.concatenate(
        [leading * cosine - trailing * sine_part, trailing * cosine + leading * sine_part], axis=-1
    )


def attend(queries, key_block, value_block):
    row_count = queries.shape[0]
    pair_local = key_block.shape[1] // HD
    group_size = queries.shape[1] // HD // pair_local
    grouped = queries.reshape(row_count, pair_local, group_size, HD)
    query_index = lax.axis_index("ctx") * row_count + jnp.arange(row_count, dtype=jnp.int32)
    score_scale = HD ** (-0.5)
    key_piece = lax.all_gather(key_block, "ctx", axis=0, tiled=True)
    value_piece = lax.all_gather(value_block, "ctx", axis=0, tiled=True)
    key_count = key_piece.shape[0]
    key_heads = key_piece.reshape(key_count, pair_local, HD)
    value_heads = value_piece.reshape(key_count, pair_local, HD)
    scores = (
        jnp.einsum("tkgd,nkd->kgtn", grouped, key_heads, preferred_element_type=jnp.float32)
        * score_scale
    )
    key_index = jnp.arange(key_count, dtype=jnp.int32)
    allowed = key_index[None, :] <= query_index[:, None]
    scores = jnp.where(allowed, scores, neg_large)
    running = jnp.full((pair_local, group_size, row_count), neg_large, jnp.float32)
    newest = jnp.maximum(running, jnp.max(scores, axis=-1))
    probs = jnp.where(allowed, jnp.exp(scores - newest[..., None]), 0.0)
    denominator = jnp.sum(probs, axis=-1)
    accum = jnp.einsum(
        "kgtn,nkd->kgtd",
        probs.astype(jnp.bfloat16),
        value_heads,
        preferred_element_type=jnp.float32,
    )
    running, denominator, accum = (newest, denominator, accum)
    result = accum / denominator[..., None]
    return result.transpose(2, 0, 1, 3).reshape(row_count, -1).astype(jnp.bfloat16)


def project(row_block, weights):
    row_total = row_block.shape[0]
    shard_count = lax.axis_size("ctx")
    tensor_count = lax.axis_size("tp")
    widths = [matrix.shape[1] for matrix in weights]
    width_sum = sum(widths)
    combined = weights[0] if len(weights) == 1 else jnp.concatenate(weights, axis=1)
    update = jnp.dot(
        row_block,
        lax.all_gather(combined, "ctx", axis=1, tiled=True),
        preferred_element_type=jnp.float32,
    )
    arranged = update.reshape(row_total, shard_count, width_sum)
    member_blocks = []
    offset = 0
    for width in widths:
        member = arranged[:, :, offset : offset + width].reshape(
            row_total, tensor_count, shard_count * width // tensor_count
        )
        member_blocks.append(member)
        offset += width
    stacked = jnp.concatenate(member_blocks, axis=2).reshape(row_total, -1)
    own_share = lax.psum_scatter(stacked, "tp", scatter_dimension=1, tiled=True)
    results = []
    offset = 0
    for width in widths:
        share_width = shard_count * width // tensor_count
        results.append(own_share[:, offset : offset + share_width])
        offset += share_width
    return results


def relocate(row_block, source, first_row):
    row_total = row_block.shape[0]
    shard_count = lax.axis_size("ctx")
    local_index = source - first_row
    present = (local_index >= 0) & (local_index < row_total)
    picked = jnp.take(row_block, jnp.clip(local_index, 0, row_total - 1), axis=0)
    outgoing = jnp.where(present[:, None], picked, jnp.zeros_like(picked))
    incoming = lax.all_to_all(outgoing, "ctx", split_axis=0, concat_axis=0, tiled=True)
    slot_count = incoming.shape[0] // shard_count
    return jnp.sum(
        incoming.reshape(shard_count, slot_count, -1).astype(jnp.float32), axis=0
    ).astype(jnp.bfloat16)


def on_device(
    query_rows,
    key_rows,
    value_rows,
    residual,
    out_weight,
    norm_gain,
    query_weight,
    key_value_weight,
    token_types,
    keep_list,
    position_ids,
):
    shard_count = lax.axis_size("ctx")
    shard_index = lax.axis_index("ctx")
    local_rows = query_rows.shape[0]
    kept_flags = ((token_types == 0) | (keep_list == 1)).astype(jnp.int32)
    running_count = jnp.cumsum(kept_flags)
    slot_numbers = jnp.arange(KEPT_DEV * shard_count, dtype=jnp.int32) + 1
    source = jnp.searchsorted(running_count, slot_numbers, side="left")
    attended = attend(query_rows, key_rows, value_rows)
    first_row = shard_index * local_rows
    summed = project(attended, [out_weight])[0]
    hidden = (residual.astype(jnp.float32) + summed).astype(jnp.bfloat16)
    kept_resid = relocate(hidden, source, first_row)
    squares = lax.psum(jnp.sum(jnp.square(kept_resid.astype(jnp.float32)), axis=1), "tp")
    normed = (
        kept_resid.astype(jnp.float32)
        * lax.rsqrt(squares[:, None] / D + 1e-06)
        * norm_gain.astype(jnp.float32)[None, :]
    ).astype(jnp.bfloat16)
    query_proj, pair_proj = project(normed, [query_weight, key_value_weight])
    kept_count = normed.shape[0]
    own_source = lax.dynamic_slice_in_dim(source, shard_index * kept_count, kept_count)
    angles = rope_angles(jnp.take(position_ids, own_source, axis=1))
    query_three = (
        rotate(query_proj.reshape(kept_count, -1, HD), angles)
        .reshape(kept_count, -1)
        .astype(jnp.bfloat16)
    )
    pair_heads = pair_proj.reshape(kept_count, -1, 2, HD)
    key_three = rotate(pair_heads[:, :, 0], angles).reshape(kept_count, -1).astype(jnp.bfloat16)
    value_three = pair_heads[:, :, 1].reshape(kept_count, -1).astype(jnp.bfloat16)
    return (kept_resid, attend(query_three, key_three, value_three))

MESH = pl.DeviceIdType.MESH
N = 4


def shifted(index, step):
    return lax.rem(index + step, N)


def block_of(index, size):
    return pl.ds(pl.multiple_of(index * size, size), size)


def softmax_pair(queries, keys, values, allowed):
    scores = lax.dot_general(
        queries, keys, (((1,), (1,)), ((), ())), preferred_element_type=jnp.float32
    ) * (HD ** (-0.5))
    scores = jnp.where(allowed, scores, neg_large)
    probs = jnp.exp(scores - jnp.max(scores, axis=1, keepdims=True))
    denominator = jnp.sum(probs, axis=1, keepdims=True)
    gained = jnp.dot(probs.astype(jnp.bfloat16), values, preferred_element_type=jnp.float32)
    return (gained / denominator).astype(jnp.bfloat16)


def fused_kernel(
    query_ref, key_ref, value_ref, resid_ref, out_w_ref, gain_ref, query_w_ref, pair_w_ref,
    types_hbm, keep_hbm, pos_hbm,
    out_ref,
    q_all, k_all, v_all, r_in, out_w, query_w, pair_w, pick, cos_s, sin_s,
    att_all, part, part_b, part_in, hid_own, hid_all,
    q_part, pair_part, sq_part, q_in, pair_in, sq_in, o_own, o_in,
    types_ref, keep_ref, pos_ref,
    w_sem, own_sem, s1, r1, s_res, r_res, s2, r2, s3, r3, s4, r4, s5, r5, s6, r6,
):
    g, c, t = lax.axis_index("groups"), lax.axis_index("ctx"), lax.axis_index("tp")
    rows = query_ref.shape[0]
    tokens = q_all.shape[0]
    kept = pick.shape[0]
    share = kept // N
    f32, bf16 = jnp.float32, jnp.bfloat16

    def send(source, target, s_sem, r_sem, cc, tt):
        return pltpu.make_async_remote_copy(
            src_ref=source, dst_ref=target, send_sem=s_sem, recv_sem=r_sem,
            device_id=(g, cc, tt), device_id_type=MESH,
        )

    barrier = pltpu.get_barrier_semaphore()
    for dc in range(N):
        for dt in range(N):
            if dc or dt:
                pl.semaphore_signal(
                    barrier, inc=1, device_id=(g, shifted(c, dc), shifted(t, dt)),
                    device_id_type=MESH,
                )
    weights = [
        pltpu.make_async_copy(a, b, w_sem.at[i])
        for i, (a, b) in enumerate([(out_w_ref, out_w), (query_w_ref, query_w), (pair_w_ref, pair_w)])
    ]
    here = block_of(c, rows)
    arrays = [(query_ref, q_all, 2 * HD, 1), (key_ref, k_all, HD, 2), (value_ref, v_all, HD, 2)]
    own = [
        pltpu.make_async_copy(a.at[:, block_of(c // div, width)], b.at[here], own_sem.at[i])
        for i, (a, b, width, div) in enumerate(arrays)
    ]
    small = [
        pltpu.make_async_copy(a, b, own_sem.at[4 + i])
        for i, (a, b) in enumerate([(types_hbm, types_ref), (keep_hbm, keep_ref), (pos_hbm, pos_ref)])
    ]
    for copy in own + small:
        copy.start()
    pl.semaphore_wait(barrier, N * N - 1)

    first = []
    for d in (2, 1, 3):
        to = shifted(c, d)
        for i, (a, b, width, div) in enumerate(arrays):
            first.append(send(
                a.at[:, block_of(to // div, width)], b.at[here],
                s1.at[3 * (d - 1) + i], r1.at[3 * (d - 1) + i], to, t,
            ))
            first[-1].start()
    resid_copy = send(resid_ref, r_in, s_res, r_res, t, c)

    @pl.when(t != c)
    def _():
        resid_copy.start()

    resid_own = pltpu.make_async_copy(resid_ref, r_in, own_sem.at[3])

    @pl.when(t == c)
    def _():
        resid_own.start()

    for copy in weights:
        copy.start()

    for copy in small:
        copy.wait()
    flags = jnp.where((types_ref[...] == 0) | (keep_ref[...] == 1), 1.0, 0.0)
    before = lax.broadcasted_iota(jnp.int32, (tokens, tokens), 0) <= lax.broadcasted_iota(
        jnp.int32, (tokens, tokens), 1
    )
    counts = jnp.dot(
        jnp.broadcast_to(flags, (16, tokens)).astype(bf16),
        jnp.where(before, 1.0, 0.0).astype(bf16),
        preferred_element_type=f32,
    )[0:1]
    place = lax.broadcasted_iota(jnp.int32, (kept, tokens), 0).astype(f32) + 1.0
    chosen = jnp.where((counts == place) & (flags > 0.5), 1.0, 0.0)
    pick[...] = chosen.astype(bf16)
    token = lax.broadcasted_iota(jnp.int32, (kept, tokens), 1)
    source = jnp.sum(chosen * token.astype(f32), axis=1, keepdims=True)
    lane = lax.broadcasted_iota(jnp.int32, (1, HD), 1)
    freq = lax.rem(lane, HD // 2).astype(f32)
    inverse = jnp.exp(freq * (-2.0 * math.log(1000000.0) / HD))
    at = [
        jnp.sum(chosen * pos_ref[i : i + 1, :].astype(f32), axis=1, keepdims=True) for i in range(3)
    ]
    angle = jnp.where(freq < HD // 8, at[0], jnp.where(freq < HD // 8 + 3 * HD // 16, at[1], at[2]))
    angle = angle * inverse
    cos_s[...] = jnp.cos(angle)
    sin_s[...] = jnp.where(lane < HD // 2, -1.0, 1.0) * jnp.sin(angle)
    allowed = token.astype(f32) <= source
    allowed = jnp.concatenate([allowed, allowed], axis=0)

    for copy in own:
        copy.wait()
    for copy in first:
        copy.wait_recv()
    queries = jnp.dot(pick[...], q_all[...], preferred_element_type=f32).astype(bf16)
    queries = jnp.concatenate([queries[:, :HD], queries[:, HD:]], axis=0)
    attended = softmax_pair(queries, k_all[...], v_all[...], allowed)
    att_all[c, :, :HD] = attended[:kept]
    att_all[c, :, HD:] = attended[kept:]

    second = []
    for d in (2, 1, 3):
        second.append(send(att_all.at[c], att_all.at[c], s2.at[d - 1], r2.at[d - 1], shifted(c, d), t))
        second[-1].start()

    @pl.when(t != c)
    def _():
        resid_copy.wait_recv()

    @pl.when(t == c)
    def _():
        resid_own.wait()

    weights[0].wait()
    part[...] = jnp.dot(pick[:, block_of(t, rows)], r_in[...], preferred_element_type=f32)
    part[...] += jnp.dot(att_all[c], out_w[block_of(c, 2 * HD), :], preferred_element_type=f32)
    for copy, d in zip(second, (2, 1, 3)):
        copy.wait_recv()
    for d in (1, 3, 2):
        other = shifted(c, N - d)
        part[...] += jnp.dot(att_all[other], out_w[block_of(other, 2 * HD), :], preferred_element_type=f32)
    part_b[...] = part[...].astype(bf16)

    third = []
    for d in (2, 3, 1):
        to = shifted(t, d)
        third.append(send(part_b.at[block_of(to, share)], part_in.at[d - 1], s3.at[d - 1], r3.at[d - 1], c, to))
        third[-1].start()
    hidden = part[block_of(t, share), :]
    for copy in third:
        copy.wait_recv()
    for d in range(N - 1):
        hidden = hidden + part_in[d].astype(f32)
    hid_own[...] = hidden.astype(bf16)

    fourth = []
    for d in range(N):
        to = shifted(c, d)
        fourth.append(send(hid_own, hid_all.at[t], s4.at[d], r4.at[t], to, c))
    for d in (2, 1, 3):
        fourth[d].start()

    @pl.when(t != c)
    def _():
        fourth[0].start()

    @pl.when(t == c)
    def _():
        hid_all[t] = hid_own[...]

    weights[1].wait()
    weights[2].wait()
    for k in range(N):
        @pl.when((t != c) | (t != k))
        def _(k=k):
            send(hid_own, hid_all.at[k], s4.at[k], r4.at[k], c, t).wait_recv()

    out_ref[0] = hid_all[c]
    resid = hid_all[...].reshape(kept, hid_all.shape[2]).astype(f32)
    scaled = (resid * gain_ref[...].astype(f32).reshape(1, -1)).astype(bf16)
    squares = jnp.sum(jnp.square(resid), axis=1, keepdims=True)
    sq_part[...] = jnp.broadcast_to(squares, (kept, HD)).T[:8]
    projected = jnp.dot(scaled, pair_w[...], preferred_element_type=f32).astype(bf16)
    for i in range(2):
        pair_part[i] = projected[:, 2 * HD * i : 2 * HD * (i + 1)]

    fifth = []

    def start_fifth(i, array, target):
        for d in (2, 3, 1):
            to = shifted(t, d)
            at = 3 * (d - 1) + i
            fifth.append(send(array(to), target.at[d - 1], s5.at[at], r5.at[at], c, to))
            fifth[-1].start()

    start_fifth(1, lambda to: pair_part.at[to // 2], pair_in)
    start_fifth(2, lambda to: sq_part, sq_in)
    projected = jnp.dot(scaled, query_w[...], preferred_element_type=f32).astype(bf16)
    for i in range(N):
        q_part[i] = projected[:, 2 * HD * i : 2 * HD * (i + 1)]
    start_fifth(0, lambda to: q_part.at[to], q_in)
    query = q_part[t].astype(f32)
    pair = pair_part[t // 2].astype(f32)
    squares = sq_part[...]
    for copy in fifth:
        copy.wait_recv()
    for d in range(N - 1):
        query = query + q_in[d].astype(f32)
        pair = pair + pair_in[d].astype(f32)
        squares = squares + sq_in[d]
    total = jnp.broadcast_to(squares[0:1], (kept, HD)).T
    scale = lax.rsqrt(total / D + 1e-06)
    cosine, sine = cos_s[...] * scale, sin_s[...] * scale

    def turned(head):
        return (head * cosine + pltpu.roll(head, HD // 2, 1) * sine).astype(bf16)

    queries = jnp.concatenate([turned(query[:, :HD]), turned(query[:, HD:])], axis=0)
    row = lax.broadcasted_iota(jnp.int32, (kept, kept), 0)
    column = lax.broadcasted_iota(jnp.int32, (kept, kept), 1)
    causal = column <= row
    causal = jnp.concatenate([causal, causal], axis=0)
    values = (pair[:, HD:] * scale).astype(bf16)
    attended = softmax_pair(queries, turned(pair[:, :HD]), values, causal)
    o_own[:, :HD] = attended[:kept]
    o_own[:, HD:] = attended[kept:]

    sixth = []
    for d in range(N):
        to = shifted(c, d)
        sixth.append(send(o_own.at[block_of(to, share)], o_in.at[t], s6.at[d], r6.at[t], to, c))
    for d in (2, 1, 3):
        sixth[d].start()

    @pl.when(t != c)
    def _():
        sixth[0].start()

    @pl.when(t == c)
    def _():
        o_in[t] = o_own[block_of(c, share), :]

    for copies in (first, second, third, fifth, fourth[1:], sixth[1:]):
        for copy in copies:
            copy.wait_send()

    @pl.when(t != c)
    def _():
        resid_copy.wait_send()
        fourth[0].wait_send()
        sixth[0].wait_send()

    for k in range(N):
        @pl.when((t != c) | (t != k))
        def _(k=k):
            send(o_own.at[block_of(c, share)], o_in.at[k], s6.at[k], r6.at[k], c, t).wait_recv()

        out_ref[1, :, 2 * HD * k : 2 * HD * (k + 1)] = o_in[k]


def fused(
    query_rows, key_rows, value_rows, residual, out_weight, norm_gain, query_weight,
    key_value_weight, token_types, keep_list, position_ids,
):
    rows, width = query_rows.shape
    tokens = rows * N
    kept = KEPT_DEV * N
    bf16, f32 = jnp.bfloat16, jnp.float32
    dma = pltpu.SemaphoreType.DMA
    vmem, anywhere = pl.BlockSpec(memory_space=pltpu.VMEM), pl.BlockSpec(memory_space=pl.ANY)
    scratch = [
        ((tokens, 2 * HD), bf16), ((tokens, HD), bf16), ((tokens, HD), bf16), (residual.shape, bf16),
        (out_weight.shape, bf16), (query_weight.shape, bf16), (key_value_weight.shape, bf16),
        ((kept, tokens), bf16), ((kept, HD), f32), ((kept, HD), f32),
        ((N, kept, 2 * HD), bf16), ((kept, width), f32), ((kept, width), bf16),
        ((N - 1, KEPT_DEV, width), bf16), ((KEPT_DEV, width), bf16), ((N, KEPT_DEV, width), bf16),
        ((N, kept, 2 * HD), bf16), ((2, kept, 2 * HD), bf16), ((8, HD), f32),
        ((N - 1, kept, 2 * HD), bf16), ((N - 1, kept, 2 * HD), bf16), ((N - 1, 8, HD), f32),
        ((kept, 2 * HD), bf16), ((N, KEPT_DEV, 2 * HD), bf16),
        ((1, tokens), jnp.int32), ((1, tokens), jnp.int32), ((3, tokens), jnp.int32),
    ]
    counts = [(3,), (7,), (9,), (9,), (), (), (3,), (3,), (3,), (3,), (4,), (4,), (9,), (9,), (4,), (4,)]
    both = pl.pallas_call(
        fused_kernel,
        out_shape=jax.ShapeDtypeStruct((2, KEPT_DEV, width), bf16),
        in_specs=[anywhere] * 5 + [vmem] + [anywhere] * 5,
        out_specs=vmem,
        scratch_shapes=[pltpu.VMEM(s, d) for s, d in scratch]
        + [dma(n) if n else dma for n in counts],
        compiler_params=pltpu.CompilerParams(
            collective_id=0, has_side_effects=True, vmem_limit_bytes=62 * 1024 * 1024
        ),
    )(
        query_rows, key_rows, value_rows, residual, out_weight, norm_gain,
        query_weight, key_value_weight, token_types.reshape(1, -1), keep_list.reshape(1, -1),
        position_ids,
    )
    return both[0], both[1]


def solution(mesh):
    in_specs = (
        P(("groups", "ctx"), "tp"),
        P(("groups", "ctx"), "tp"),
        P(("groups", "ctx"), "tp"),
        P(("groups", "ctx"), "tp"),
        P("tp", "ctx"),
        P("tp"),
        P("tp", "ctx"),
        P("tp", "ctx"),
        P("groups"),
        P("groups"),
        P(None, "groups"),
    )
    out_specs = (P(("groups", "ctx"), "tp"), P(("groups", "ctx"), "tp"))
    whole_heads = mesh.shape["ctx"] == N and mesh.shape["tp"] == N
    return jax.shard_map(
        fused if whole_heads else on_device, mesh=mesh, in_specs=in_specs, out_specs=out_specs, check_vma=False
    )
```
